256 devices in a mesh: wide: 64 (over x_lo, y, z), narrow: 4 (over x_hi, core).
Axes of the slice: x: 4 (x_hi: 2, x_lo: 2; x = x_hi * 2 + x_lo), y: 4, z: 8, core: 2. Of those that a mesh axis runs over, the one named last changes fastest.
Arguments:
- query_in: bfloat16 [8, 32, 14336], P(None, None, 'narrow'), may hold values from -1.0546875 to 1.0546875
- query_out: bfloat16 [8, 32, 4096], replicated, may hold values from -6 to 6
- train_in: bfloat16 [64, 32, 14336], P('wide', None, 'narrow'), may hold values from -6 to 6
- train_out: bfloat16 [64, 32, 4096], P('wide'), may hold values from -6 to 6
- basis_in: bfloat16 [14336, 14336], P('wide', 'narrow'), may hold values from -0.046875 to 0.046875
- basis_out: bfloat16 [4096, 4096], P('narrow', 'wide'), may hold values from -0.09375 to 0.09375
- eigvals: float32 [4096, 14336], P('narrow', 'wide'), may hold values from 0.02 to 40
Outputs:
- precond: bfloat16 [8, 4096, 14336], P(None, 'narrow', 'wide')
- scores: float32 [8, 64], replicated
The draws below stay inside these ranges and needn't reach their ends.
All inputs are finite; a program needn't handle non-finite values.
Results may differ from the reference program's by a relative error of at most 0.0057.
Values may be sent and summed in bfloat16 or wider, within the bound.
A program may use at most 128 MiB of HBM per device.

```python
import jax
import jax.numpy as jnp
from jax import lax

DS = 4096
DA = 14336
RANK = 32
QRANK = 32
QRY = 8
TRAIN = 64


def draw_eigvals(key, part):
    key = jax.random.fold_in(key, 11)
    row_pos = jnp.arange(DS, dtype=jnp.float32)[:, None] / DS
    col_pos = jnp.arange(DA, dtype=jnp.float32)[None, :] / DA
    base = jnp.power(10.0, 1.0 - 1.5 * col_pos - 0.5 * row_pos)
    rough = jnp.exp(jax.random.uniform(key, (DS, DA), jnp.float32, -0.69, 0.69))
    return (base * rough).astype(jnp.float32)


def block_levels(stream_key, extent, shards, least, top_value):
    def one(position, parts):
        draws = jax.random.uniform(jax.random.fold_in(jax.random.fold_in(stream_key, 6), position), (parts,), jnp.float32, least / len(shards), top_value / len(shards))
        return jnp.repeat(jnp.exp(draws), extent[position] // parts).reshape((-1,) + (1,) * (len(extent) - position - 1))

    level = one(*shards[0])
    for cut in shards[1:]:
        level = level * one(*cut)
    return level


def gaussian(rng, shape, spread, bound, cuts=(), kind=jnp.bfloat16):
    loudness = block_levels(rng, shape, cuts, -0.22, 0.18) if cuts else 1.0
    entries = jax.random.normal(rng, shape, jnp.float32) * spread * loudness
    return jnp.minimum(jnp.maximum(entries, -bound), bound).astype(kind)


def setup_inputs(seed: int = 0) -> dict:
    key_of = jax.random.split(jax.random.key(seed), 8)
    return {
        "query_in": gaussian(key_of[0], (QRY, QRANK, DA), (QRANK ** -0.5), 1.0546875, ((2, 4),)),
        "query_out": gaussian(key_of[1], (QRY, QRANK, DS), 1.0, 6.0),
        "train_in": gaussian(key_of[2], (TRAIN, RANK, DA), 1.0, 6.0, ((0, 64), (2, 4))),
        "train_out": gaussian(key_of[3], (TRAIN, RANK, DS), 1.0, 6.0, ((0, 64),)),
        "basis_in": gaussian(key_of[4], (DA, DA), DA ** -0.5, 0.046875, ((0, 64), (1, 4))),
        "basis_out": gaussian(key_of[5], (DS, DS), DS ** -0.5, 0.09375, ((0, 4), (1, 64))),
        "eigvals": draw_eigvals(jax.random.fold_in(key_of[7], 71), 0),
    }


def reference(query_in, query_out, train_in, train_out, basis_in, basis_out, eigvals):
    damping = 0.1 * jnp.sum(eigvals) / (DS * DA)
    query_rot = jnp.dot(query_in.reshape(QRY * QRANK, DA), basis_in.T, preferred_element_type=jnp.float32).astype(jnp.bfloat16).reshape(QRY, QRANK, DA)
    train_rot = jnp.dot(train_in.reshape(TRAIN * RANK, DA), basis_in.T, preferred_element_type=jnp.float32).astype(jnp.bfloat16)
    query_side = jnp.dot(query_out.reshape(QRY * QRANK, DS), basis_out.T, preferred_element_type=jnp.float32).astype(jnp.bfloat16).reshape(QRY, QRANK, DS)
    train_side = jnp.dot(train_out.reshape(TRAIN * RANK, DS), basis_out.T, preferred_element_type=jnp.float32).astype(jnp.bfloat16)
    train_wide = train_side.astype(jnp.float32)

    def one_query(operands):
        side_q, rot_q = operands
        product = jnp.dot(side_q.T, rot_q, preferred_element_type=jnp.float32)
        scaled = (product / (eigvals + damping)).astype(jnp.bfloat16)
        projected = jnp.dot(train_rot, scaled.T, preferred_element_type=jnp.float32)
        per_pair = lax.optimization_barrier(jnp.sum(projected * train_wide, axis=1))
        return (scaled, lax.optimization_barrier(jnp.sum(per_pair.reshape(TRAIN, RANK), axis=1)))
    precond, raw_scores = lax.map(one_query, (query_side, query_rot))
    scores = raw_scores / jnp.sqrt(jnp.float32(RANK * DS * DA))
    return (precond, scores)
```

```python
import jax
import jax.numpy as jnp
from jax import lax
from jax.experimental import pallas as pl
from jax.experimental.pallas import tpu as pltpu
from jax.sharding import PartitionSpec as P

DS = 4096
DA = 14336
RANK = 32
Y = 4
Z = 8
X = 4
GROUP = 8
MESH = pl.DeviceIdType.MESH
VMEM = pl.BlockSpec(memory_space=pltpu.VMEM)
ANY = pl.BlockSpec(memory_space=pl.ANY)


class Place:
    def __init__(self):
        wide = lax.axis_index("wide")
        narrow = lax.axis_index("narrow")
        self.z = lax.rem(wide, Z)
        self.y = lax.rem(wide // Z, Y)
        self.x_lo = wide // (Y * Z)
        self.x_hi = narrow // 2
        self.core = lax.rem(narrow, 2)
        self.n = narrow
        self.x = self.x_hi * 2 + self.x_lo
        self.g = self.x * 2 + self.core

    def dev(self, x_hi=None, x_lo=None, core=None, y=None, z=None):
        x_hi = self.x_hi if x_hi is None else x_hi
        x_lo = self.x_lo if x_lo is None else x_lo
        core = self.core if core is None else core
        y = self.y if y is None else y
        z = self.z if z is None else z
        return ((x_lo * Y + y) * Z + z, x_hi * 2 + core)

    def in_group(self, g):
        return self.dev(x_hi=g // 4, x_lo=lax.rem(g // 2, 2), core=lax.rem(g, 2))


def step(value, by, size):
    return lax.rem(value + (by % size), size)


def greet(devices):
    barrier = pltpu.get_barrier_semaphore()
    for device in devices:
        pl.semaphore_signal(barrier, inc=1, device_id=device, device_id_type=MESH)
    return lambda: pl.semaphore_wait(barrier, len(devices))


class Net:
    def __init__(self, me, send_sems, recv_sems):
        self.me = me
        self.send_sems = send_sems
        self.recv_sems = recv_sems
        self.sent = 0
        self.keys = {}
        self.pending = []

    def sem(self, key):
        return self.recv_sems.at[self.keys.setdefault(key, len(self.keys))]

    def send(self, src, dst, to, key, when=None):
        copy = pltpu.make_async_remote_copy(
            src_ref=src, dst_ref=dst, send_sem=self.send_sems.at[self.sent],
            recv_sem=self.sem(key), device_id=to, device_id_type=MESH,
        )
        self.sent += 1
        if when is None:
            copy.start()
        else:
            pl.when(when)(copy.start)
        self.pending.append((when, copy))
        return copy

    def arrive(self, dst, key, when=None):
        copy = pltpu.make_async_remote_copy(
            src_ref=dst, dst_ref=dst, send_sem=self.send_sems.at[0], recv_sem=self.sem(key),
            device_id=self.me.dev(core=1 - self.me.core), device_id_type=MESH,
        )
        if when is None:
            copy.wait_recv()
        else:
            pl.when(when)(copy.wait_recv)

    def finish(self):
        for when, copy in self.pending:
            if when is None:
                copy.wait_send()
            else:
                pl.when(when)(copy.wait_send)


def ups(size, odd):
    return size // 2 if odd == 0 else size - 1 - size // 2


class Gather:
    def __init__(self, net, name, buf, slot, relative=False):
        self.net, self.name, self.buf, self.slot, self.relative = net, name, buf, slot, relative

    def send(self, axis, back_y, back_z, way):
        net, me = self.net, self.net.me
        src = self.buf.at[self.slot(back_y, back_z)]
        if axis == "y":
            key = (self.name, (back_y + way) % Y, back_z % Z)
            net.send(src, src, me.dev(y=step(me.y, way, Y)), key)
        else:
            dst = self.buf.at[self.slot(back_y, back_z + way)] if self.relative else src
            key = (self.name, back_y % Y, (back_z + way) % Z)
            net.send(src, dst, me.dev(z=step(me.z, way, Z)), key)

    def arrive(self, back_y, back_z):
        key = (self.name, back_y % Y, back_z % Z)
        self.net.arrive(self.buf.at[self.slot(back_y, back_z)], key)

    def ring(self, axis, fixed, far, odd):
        size = Y if axis == "y" else Z
        up = ups(size, odd % 2)
        for way, reach in ((1, up), (-1, size - 1 - up)):
            if far > reach:
                continue
            at = (far * way, fixed) if axis == "y" else (fixed, far * way)
            if far > 0:
                self.arrive(*at)
            if far < reach:
                self.send(axis, *at, way)

    def direct_y(self):
        for back in range(1, Y):
            self.send("y", 0, 0, back)


class PairShare:
    def __init__(self, net, name, src, dst, parts):
        self.net, self.name, self.src, self.dst = net, name, src, dst
        self.half = src.shape[0] // 2
        self.width = src.shape[1] // parts
        self.parts = parts
        me = net.me
        self.home = me.x_lo == me.core
        self.away = me.x_lo != me.core
        self.relayed = []

    def rows(self, which):
        return pl.ds(which * self.half, self.half)

    def columns(self, part):
        return slice(part * self.width, part * self.width + self.width)

    def start(self, part):
        me, net = self.net.me, self.net
        columns = self.columns(part)
        for core in range(2):
            net.send(
                self.src.at[self.rows(core), columns],
                self.dst.at[me.x_lo, self.rows(core), columns],
                me.dev(x_lo=1 - me.x_lo, core=core), (self.name, part, 0), when=self.away,
            )
        net.send(
            self.src.at[:, columns], self.dst.at[me.x_lo, :, columns],
            me.dev(core=1 - me.core), (self.name, part, 1), when=self.home,
        )

    def relay(self, part):
        me, net = self.net.me, self.net
        block = self.dst.at[1 - me.x_lo, self.rows(me.core), self.columns(part)]
        net.arrive(block, (self.name, part, 0))
        self.relayed.append(net.send(block, block, me.dev(core=1 - me.core), (self.name, part, 2)))
        net.pending.pop()

    def end(self):
        me, net = self.net.me, self.net
        for part in range(self.parts):
            columns = self.columns(part)
            other = self.dst.at[1 - me.x_lo, self.rows(1 - me.core), columns]
            net.arrive(other, (self.name, part, 2))
            whole = self.dst.at[me.x_lo, :, columns]
            net.arrive(whole, (self.name, part, 1), when=self.away)
        for copy in self.relayed:
            copy.wait_send()


def position(back_z):
    back_z = back_z % Z
    return 2 * back_z - (back_z > 0) if back_z <= Z // 2 else 2 * (Z - back_z)


def nt(a, b):
    return lax.dot_general(a, b, (((1,), (1,)), ((), ())), preferred_element_type=jnp.float32)


def tn_t(a, b):
    return lax.dot_general(a, b, (((0,), (1,)), ((), ())), preferred_element_type=jnp.float32)


def spread_group(net, name, buf):
    mine = buf.at[net.me.g]
    for back in range(1, GROUP):
        net.send(mine, mine, net.me.in_group(step(net.me.g, back, GROUP)), (name, back))


def collect_group(net, name, buf):
    for back in range(1, GROUP):
        net.arrive(buf.at[step(net.me.g, -back, GROUP)], (name, back))


def spread_y(net, name, buf):
    mine = buf.at[net.me.y]
    for back in range(1, Y):
        net.send(mine, mine, net.me.dev(y=step(net.me.y, back, Y)), (name, back))


def collect_y(net, name, buf):
    for back in range(1, Y):
        net.arrive(buf.at[step(net.me.y, -back, Y)], (name, back))


def spread_z(net, name, buf):
    mine = buf.at[net.me.z]
    for back in range(1, Z):
        net.send(mine, mine, net.me.dev(z=step(net.me.z, back, Z)), (name, back))


def collect_z(net, name, buf):
    for back in range(1, Z):
        net.arrive(buf.at[step(net.me.z, -back, Z)], (name, back))


def rotate_kernel(
    train, basis, eigs, train_out, small, query_in, query_out,
    out_side, qr, eig_sum, part_sum,
    tr, sides, eigs_all, eigs_round, inverse, outer_own, outer,
    scaled, ts, pairs, f1, f2, f3,
    train_all, basis_all, outer_all, small_all, small_pad,
    basis_own, query_rows, query_cols, eigs_own,
    cpart, c_in, st, s_in, sq, sq_in, qp, qp_in, e1, e2, e3,
    send_sems, recv_sems, local_sems,
):
    bf16, f32 = jnp.bfloat16, jnp.float32
    me = Place()
    net = Net(me, send_sems, recv_sems)
    home = me.x_lo == me.core
    away = me.x_lo != me.core
    swapped = dict(x_lo=me.core, core=me.x_lo)

    loads = [
        pltpu.make_async_copy(train_out, outer_own, local_sems.at[8 + 2 * Y]),
        pltpu.make_async_copy(eigs, eigs_own, local_sems.at[5]),
        pltpu.make_async_copy(basis, basis_own, local_sems.at[6]),
        pltpu.make_async_copy(query_in, query_rows, local_sems.at[7]),
    ]
    cols_z = me.z // 2 * 128
    for part in range(2 * Y):
        offset = pl.multiple_of(part * (query_out.shape[1] // (2 * Y)) + cols_z, 128)
        loads.append(
            pltpu.make_async_copy(
                query_out.at[:, pl.ds(offset, 128)],
                query_cols.at[:, part * 128 : part * 128 + 128],
                local_sems.at[8 + part],
            )
        )
    for load in loads:
        load.start()
    partners = []
    for back in range(Y):
        for flip_x in range(2):
            for flip_core in range(2):
                if back + flip_x + flip_core > 0:
                    partners.append(
                        me.dev(
                            x_lo=1 - me.x_lo if flip_x else me.x_lo,
                            core=1 - me.core if flip_core else me.core,
                            y=step(me.y, back, Y),
                        )
                    )
    for back in range(1, Z):
        partners.append(me.dev(z=step(me.z, back, Z), **swapped))
        partners.append(me.dev(z=step(me.z, back, Z)))
    for x_lo in range(2):
        for core in range(2):
            partners.append(me.dev(x_hi=1 - me.x_hi, x_lo=x_lo, core=core))
    all_here = greet(partners)
    small_pad[...] = jnp.zeros_like(small_pad)
    loads[0].wait()
    depth = small.shape[0]
    for z in range(Z):
        pieces = []
        for part in range(2 * Y):
            first = (part * Z + z) * depth
            pieces.append(outer_own[:, first : first + depth])
        outer[z] = jnp.concatenate(pieces, axis=1)
    all_here()

    own_slot = train_all.at[0, me.y]
    own_copy = pltpu.make_async_copy(train, own_slot, local_sems.at[0])
    pl.when(home)(own_copy.start)
    net.send(train, own_slot, me.dev(**swapped), "swap", when=away)

    outer_slot = outer_all.at[me.z, me.y]
    outer_copy = pltpu.make_async_copy(outer.at[me.z], outer_slot, local_sems.at[1])
    pl.when(home)(outer_copy.start)
    net.send(outer.at[me.z], outer_slot, me.dev(**swapped), ("outer", 0), when=away)
    for back in range(1, Z):
        to_z = step(me.z, back, Z)
        net.send(outer.at[to_z], outer_slot, me.dev(z=to_z, **swapped), ("outer", back))

    width = small.shape[1] // Y
    small_slot = me.x_lo * Y + me.y

    def small_part(y):
        return small.at[:, pl.ds(pl.multiple_of(y * width, width), width)]

    small_copy = pltpu.make_async_copy(small_part(me.y), small_all.at[small_slot], local_sems.at[2])
    pl.when(home)(small_copy.start)
    for back in range(Y):
        to_y = step(me.y, back, Y)
        for core in range(2):
            pair = net.keys.setdefault(("small", back, 0), len(net.keys))
            other = net.keys.setdefault(("small", back, 1), len(net.keys))
            copy = pltpu.make_async_remote_copy(
                src_ref=small_part(to_y), dst_ref=small_all.at[small_slot],
                send_sem=net.send_sems.at[net.sent],
                recv_sem=net.recv_sems.at[pair + (other - pair) * me.x_lo],
                device_id=me.dev(x_lo=me.core, core=core, y=to_y), device_id_type=MESH,
            )
            net.sent += 1
            when = None
            if back == 0:
                when = jnp.logical_or(away, me.core != core)
                pl.when(when)(copy.start)
            else:
                copy.start()
            net.pending.append((when, copy))

    rows_q = qp.shape[0] // 4
    loads[1].wait()
    tile = jnp.sum(eigs_own[...].reshape(-1, 8, eigs_own.shape[1]), axis=0)
    e1[me.g] = sum(tile[:, 128 * part : 128 * part + 128] for part in range(tile.shape[1] // 128))
    spread_group(net, "e1", e1)
    eigs_round[...] = eigs_own[...].astype(bf16)

    pl.when(home)(own_copy.wait)
    net.arrive(own_slot, "swap", when=away)
    trains = Gather(
        net, "train", train_all,
        lambda back_y, back_z: (position(back_z), step(me.y, -back_y, Y)), relative=True,
    )

    def groups(far):
        return (far,) if far in (0, Z // 2) else (far, -far)

    def train_z(far):
        trains.ring("z", 0, far, 0)
        for back_z in groups(far):
            trains.ring("y", back_z, 0, back_z)

    def train_y(far):
        for hop in range(1, Y // 2 + 1):
            for back_z in groups(far):
                trains.ring("y", back_z, hop, back_z)

    def side_z(far):
        for back in range(Y):
            smalls.ring("z", back, far, back)

    train_z(0)
    share_basis = PairShare(net, "basis", basis, basis_all, 4)
    share_eigs = PairShare(net, "eigs", eigs_round, eigs_all, 1)

    def outer_rows():
        pl.when(home)(outer_copy.wait)
        net.arrive(outer_slot, ("outer", 0), when=away)
        for back in range(1, Z):
            net.arrive(outer_all.at[step(me.z, -back, Z), me.y], ("outer", back))
        block = outer_all.at[:, me.y]
        for back in range(1, Y):
            net.send(block, block, me.dev(y=step(me.y, back, Y)), ("outer_y", back))

    def query_parts():
        loads[2].wait()
        loads[3].wait()
        qp[...] = nt(basis_own[...], query_rows[...])
        for back in range(1, 4):
            to_n = step(me.n, back, 4)
            net.send(
                qp.at[pl.ds(to_n * rows_q, rows_q)], qp_in.at[back],
                me.dev(x_hi=to_n // 2, core=lax.rem(to_n, 2)), ("qp", back),
            )

    def place_own():
        @pl.when(home)
        def _():
            basis_all[me.x_lo] = basis_own[...]
            eigs_all[me.x_lo] = eigs_round[...]

    rows_s = st.shape[0] // Z
    cols = st.shape[1]

    def side_parts():
        pl.when(home)(small_copy.wait)
        for x_lo in range(2):
            for back in range(Y):
                slot = small_all.at[x_lo * Y + step(me.y, -back, Y)]
                if back == 0:
                    here = jnp.logical_and(home, me.x_lo == x_lo)
                    net.arrive(slot, ("small", back, x_lo), when=jnp.logical_not(here))
                else:
                    net.arrive(slot, ("small", back, x_lo))
        for load in loads[4:]:
            load.wait()
        pad_row = lax.rem(me.z, 2) * depth
        for part in range(2 * Y):
            at = pl.ds(pl.multiple_of(part * 128 + pad_row, depth), depth)
            small_pad[at, :] = small_all[part]
        sq[...] = tn_t(small_pad[...], query_cols[...])
        for back in range(1, Z):
            to_z = step(me.z, back, Z)
            part = pl.ds(pl.multiple_of(to_z * rows_s, rows_s), rows_s)
            net.send(sq.at[part], sq_in.at[back], me.dev(z=to_z), ("side_q", back))
        for back in range(1, Y):
            net.arrive(outer_all.at[:, step(me.y, -back, Y)], ("outer_y", back))
        st[...] = tn_t(
            small_all[...].reshape(-1, width), outer_all[...].reshape(-1, 2 * Y * depth)
        ).astype(bf16)
        for back in range(1, Z):
            to_z = step(me.z, back, Z)
            part = pl.ds(pl.multiple_of(to_z * rows_s, rows_s), rows_s)
            net.send(st.at[part], s_in.at[back], me.dev(z=to_z), ("side", back))

    def query_sums():
        part = pl.ds(me.n * rows_q, rows_q)
        total = qp[part]
        for back in range(1, 4):
            net.arrive(qp_in.at[back], ("qp", back))
            total += qp_in[back]
        qr[me.x_lo, part] = total
        mine = qr.at[me.x_lo, part]
        for back in range(1, GROUP):
            net.send(mine, mine, me.in_group(step(me.g, back, GROUP)), ("qr", back))

    def side_sums():
        part = pl.ds(pl.multiple_of(me.z * rows_s, rows_s), rows_s)
        total = st[part].astype(f32)
        total_q = sq[part]
        for back in range(1, Z):
            net.arrive(sq_in.at[back], ("side_q", back))
            total_q += sq_in[back]
            net.arrive(s_in.at[back], ("side", back))
            total += s_in[back].astype(f32)
        sides[me.y, me.z, :, :cols] = total.astype(bf16)
        sides[me.y, me.z, :, cols:] = total_q.astype(bf16)

    smalls = Gather(
        net, "sides", sides,
        lambda back_y, back_z: (step(me.y, -back_y, Y), step(me.z, -back_z, Z)),
    )
    rows_c = cpart.shape[0] // X
    rows_g = Y * train.shape[0]

    def lanes(batch):
        low, high = (0, 1) if batch == 0 else (2 * batch - 1, min(2 * batch + 1, Z))
        return low, high, slice(low * rows_g, high * rows_g)

    def x_part(x):
        return pl.ds(pl.multiple_of(x * rows_c, rows_c), rows_c)

    def to_x(back):
        x = step(me.x, back, X)
        return x, me.dev(x_hi=x // 2, x_lo=lax.rem(x, 2))

    def multiply(batch):
        low, high, span = lanes(batch)
        rows = train_all[low:high].reshape((high - low) * rows_g, train.shape[1])
        both = basis_all[...].reshape(-1, train.shape[1])
        cpart[:, span] = nt(both, rows).astype(bf16)
        for back in range(1, X):
            x, device = to_x(back)
            net.send(
                cpart.at[x_part(x), span], c_in.at[back, :, span], device, ("ct", batch, back)
            )

    def combine(batch):
        span = lanes(batch)[2]
        part = x_part(me.x)
        total = cpart[part, span].astype(f32)
        for back in range(1, X):
            net.arrive(c_in.at[back, :, span], ("ct", batch, back))
            total += c_in[back, :, span].astype(f32)
        tr[part, span] = total.astype(bf16)
        mine = tr.at[part, span]
        for back in range(1, X):
            net.send(mine, mine, to_x(back)[1], ("tr", batch, back))

    def swap_queries(far):
        for back_z in groups(far):
            z = step(me.z, -back_z, Z)
            net.send(
                sides.at[:, z, :, cols:], out_side.at[:, z], me.dev(**swapped),
                ("swap_q", back_z % Z), when=away,
            )

    def score(batches):
        for batch in batches:
            for back in range(1, X):
                part = x_part(step(me.x, -back, X))
                net.arrive(tr.at[part, lanes(batch)[2]], ("tr", batch, back))
        span = slice(lanes(batches[0])[2].start, lanes(batches[-1])[2].stop)

        def one(query, carry):
            projected = jnp.dot(scaled[query], ts[:, span], preferred_element_type=f32)
            product = projected * tr[:, span].astype(f32)
            pairs[query, :, span] = jnp.sum(product.reshape(-1, 8, product.shape[1]), axis=0)
            return carry

        lax.fori_loop(0, pairs.shape[0], one, 0, unroll=2)

    def pick(block, query):
        lane = lax.broadcasted_iota(jnp.int32, block.shape, 1)
        keep = jnp.logical_and(lane >= query * RANK, lane < (query + 1) * RANK)
        return jnp.where(keep, block, 0.0).astype(bf16)

    def scale(query, carry):
        left = pick(qr[...].reshape(-1, qr.shape[2]), query)
        product = nt(left, sides[:, :, :, cols:].reshape(-1, qr.shape[2]))
        scaled[query] = (product * inverse[...].reshape(product.shape)).astype(bf16)
        return carry

    outer_rows()
    share_basis.start(0)
    train_z(1)
    query_parts()
    train_z(2)
    side_parts()
    train_z(3)
    share_basis.start(1)
    query_sums()
    collect_group(net, "e1", e1)
    e2[me.y] = jnp.sum(e1[...], axis=0)
    spread_y(net, "e2", e2)
    train_z(4)
    share_basis.start(2)
    share_basis.start(3)
    side_sums()
    smalls.direct_y()
    smalls.ring("z", 0, 0, 0)
    place_own()
    train_y(0)
    share_eigs.start(0)
    for back in range(1, Y):
        smalls.arrive(back, 0)
        smalls.ring("z", back, 0, back)
    swap_queries(0)
    train_y(1)
    side_z(1)
    swap_queries(1)
    share_basis.relay(0)
    share_basis.relay(1)
    collect_y(net, "e2", e2)
    e3[me.z] = jnp.sum(e2[...], axis=0)
    spread_z(net, "e3", e3)
    side_z(2)
    swap_queries(2)
    share_basis.relay(2)
    share_basis.relay(3)
    train_y(2)
    side_z(3)
    swap_queries(3)
    share_basis.end()
    multiply(0)
    multiply(1)
    side_z(4)
    swap_queries(4)
    share_eigs.relay(0)
    multiply(2)
    combine(0)
    train_y(3)
    multiply(3)
    combine(1)
    collect_z(net, "e3", e3)
    eig_sum[...] = jnp.sum(e3[...], axis=0)
    damp = (0.1 / (DS * DA)) * jnp.sum(eig_sum[...])
    for back in range(1, GROUP):
        g = step(me.g, -back, GROUP)
        n = (g // 4) * 2 + lax.rem(g, 2)
        net.arrive(qr.at[lax.rem(g // 2, 2), pl.ds(n * rows_q, rows_q)], ("qr", back))
    share_eigs.end()
    inverse[...] = 1.0 / (eigs_all[...].astype(f32) + damp)
    queries = pairs.shape[0]
    lax.fori_loop(0, queries // 2, scale, 0, unroll=2)
    train_y(4)
    multiply(4)
    combine(2)
    combine(3)
    lax.fori_loop(queries // 2, queries, scale, 0, unroll=2)
    combine(4)
    for back in range(Z):
        at = position(back) * rows_g
        start = pl.multiple_of(step(me.z, -back, Z) * rows_g, rows_g)
        ts[:, at : at + rows_g] = sides[:, :, :, pl.ds(start, rows_g)].reshape(-1, rows_g)
    score((0, 1, 2))
    score((3, 4))

    rows = tr.shape[1]
    row = lax.broadcasted_iota(jnp.int32, (rows, 128), 0)
    lane = lax.broadcasted_iota(jnp.int32, (rows, 128), 1)
    place = row // rows_g
    back = jnp.where(place % 2 == 1, (place + 1) // 2, Z - place // 2)
    z = (me.z + Z - back) % Z
    sample = (me.core * Y + (row % rows_g) // RANK) * Z + z
    sums = jnp.dot(
        pairs[...].reshape(-1, rows), jnp.where(lane == sample, 1.0, 0.0),
        preferred_element_type=f32, precision=lax.Precision.HIGHEST,
    )
    f1[me.g] = jnp.sum(sums.reshape(-1, 8, 128), axis=1)
    spread_group(net, "f1", f1)

    collect_group(net, "f1", f1)
    f2[me.y] = jnp.sum(f1[...], axis=0)
    spread_y(net, "f2", f2)
    collect_y(net, "f2", f2)
    f3[me.z] = jnp.sum(f2[...], axis=0)
    spread_z(net, "f3", f3)
    for back_z in range(Z):
        net.arrive(out_side.at[:, step(me.z, -back_z, Z)], ("swap_q", back_z), when=away)

    @pl.when(home)
    def _():
        out_side[...] = sides[:, :, :, cols:]

    collect_z(net, "f3", f3)
    part_sum[...] = jnp.sum(f3[...], axis=0)
    net.finish()


def precond_kernel(out_side, qr, eig_sum, part_sum, eigs, precond, scores, inv):
    turn = pl.program_id(0)
    x_lo = Place().x_lo
    each = precond.shape[0]

    @pl.when(turn == 0)
    def _():
        damp = (0.1 / (DS * DA)) * jnp.sum(eig_sum[...])
        inv[...] = 1.0 / (eigs[...] + damp)
        total = part_sum[:, : scores.shape[1]]
        scores[...] = total / jnp.sqrt(jnp.float32(RANK * DS * DA))

    for sub in range(each):
        query = turn * each + sub
        block = qr[x_lo]
        lane = lax.broadcasted_iota(jnp.int32, block.shape, 1)
        keep = jnp.logical_and(lane >= query * RANK, lane < (query + 1) * RANK)
        left = jnp.where(keep, block, 0.0).astype(jnp.bfloat16)
        precond[sub] = (nt(left, out_side[...]) * inv[...]).astype(jnp.bfloat16)


def precondition(out_side, qr, eig_sum, part_sum, eigs):
    queries = part_sum.shape[0]
    each = 2
    return pl.pallas_call(
        precond_kernel,
        grid=(queries // each,),
        out_shape=(
            jax.ShapeDtypeStruct((queries,) + eigs.shape, jnp.bfloat16),
            jax.ShapeDtypeStruct((queries, 2 * Y * Z), jnp.float32),
        ),
        in_specs=[VMEM] * 5,
        out_specs=(
            pl.BlockSpec((each,) + eigs.shape, lambda q: (q, 0, 0)),
            pl.BlockSpec((queries, 2 * Y * Z), lambda q: (0, 0)),
        ),
        scratch_shapes=[pltpu.VMEM(eigs.shape, jnp.float32)],
        compiler_params=pltpu.CompilerParams(vmem_limit_bytes=12 << 20),
        name="precondition",
    )(out_side, qr, eig_sum, part_sum, eigs)


def influence(train, basis, eigs, train_out, small, query_in, query_out, queries):
    bf16, f32 = jnp.bfloat16, jnp.float32
    rank, coords = train.shape
    block = basis.shape[0]
    wide = small.shape[1]
    width = wide // Y
    rows = Y * Z * rank
    query_rows = query_in.shape[0]
    rows_s = width // Z
    outer = (Z, rank, train_out.shape[1] // Z)
    return pl.pallas_call(
        rotate_kernel,
        out_shape=(
            jax.ShapeDtypeStruct((Y, Z, rows_s, query_rows), bf16),
            jax.ShapeDtypeStruct((2, block, query_rows), f32),
            jax.ShapeDtypeStruct((8, 128), f32),
            jax.ShapeDtypeStruct((queries, 128), f32),
        ),
        in_specs=[ANY] * 7,
        out_specs=[VMEM] * 4,
        scratch_shapes=[
            pltpu.VMEM((2 * block, rows), bf16),
            pltpu.VMEM((Y, Z, rows_s, rows + query_rows), bf16),
            pltpu.VMEM((2,) + eigs.shape, bf16),
            pltpu.VMEM(eigs.shape, bf16),
            pltpu.VMEM((2,) + eigs.shape, f32),
            pltpu.VMEM(train_out.shape, bf16),
            pltpu.VMEM(outer, bf16),
            pltpu.VMEM((queries, 2 * block, wide), bf16),
            pltpu.VMEM((wide, rows), bf16),
            pltpu.VMEM((queries, 8, rows), f32),
            pltpu.VMEM((GROUP, 8, 128), f32),
            pltpu.VMEM((Y, 8, 128), f32),
            pltpu.VMEM((Z, 8, 128), f32),
            pltpu.VMEM((Z, Y, rank, coords), bf16),
            pltpu.VMEM((2, block, coords), bf16),
            pltpu.VMEM((Z, Y) + outer[1:], bf16),
            pltpu.VMEM((2 * Y, small.shape[0], width), bf16),
            pltpu.VMEM((2 * Y * 128, width), bf16),
            pltpu.VMEM(basis.shape, bf16),
            pltpu.VMEM(query_in.shape, bf16),
            pltpu.VMEM((query_rows, 2 * Y * 128), bf16),
            pltpu.VMEM(eigs.shape, f32),
            pltpu.VMEM((2 * block, rows), bf16),
            pltpu.VMEM((X, 2 * block // X, rows), bf16),
            pltpu.VMEM((width, rows), bf16),
            pltpu.VMEM((Z, rows_s, rows), bf16),
            pltpu.VMEM((width, query_rows), f32),
            pltpu.VMEM((Z, rows_s, query_rows), f32),
            pltpu.VMEM((block, query_rows), f32),
            pltpu.VMEM((4, block // 4, query_rows), f32),
            pltpu.VMEM((GROUP, 8, 128), f32),
            pltpu.VMEM((Y, 8, 128), f32),
            pltpu.VMEM((Z, 8, 128), f32),
            pltpu.SemaphoreType.DMA((288,)),
            pltpu.SemaphoreType.DMA((288,)),
            pltpu.SemaphoreType.DMA((9 + 2 * Y,)),
        ],
        compiler_params=pltpu.CompilerParams(
            collective_id=0, has_side_effects=True, vmem_limit_bytes=58 << 20
        ),
        name="influence",
    )(train, basis, eigs, train_out, small, query_in, query_out)


def shards(query_in, query_out, train_in, train_out, basis_in, basis_out, eigvals):
    queries, qrank, coords = query_in.shape
    eigs = eigvals.T
    out_side, qr, eig_sum, part_sum = influence(
        train_in[0], basis_in, eigs, train_out[0], basis_out.T,
        query_in.reshape(queries * qrank, coords),
        query_out.reshape(queries * qrank, query_out.shape[2]), queries,
    )
    precond, scores = precondition(
        out_side.reshape(-1, out_side.shape[3]), qr, eig_sum, part_sum, eigs
    )
    return precond.transpose(0, 2, 1), scores


def solution(mesh):
    placed = (
        P(None, None, "narrow"),
        P(),
        P("wide", None, "narrow"),
        P("wide", None, None),
        P("wide", "narrow"),
        P("narrow", "wide"),
        P("narrow", "wide"),
    )
    return jax.shard_map(
        shards,
        mesh=mesh,
        in_specs=placed,
        out_specs=(P(None, "narrow", "wide"), P()),
        check_vma=False,
    )
```

```python
import jax
import jax.numpy as jnp
from jax import lax
from jax.experimental import pallas as pl
from jax.experimental.pallas import tpu as pltpu
from jax.sharding import PartitionSpec as P

DS = 4096
DA = 14336
RANK = 32
Y = 4
Z = 8
X = 4
GROUP = 8
MESH = pl.DeviceIdType.MESH
VMEM = pl.BlockSpec(memory_space=pltpu.VMEM)
ANY = pl.BlockSpec(memory_space=pl.ANY)


class Place:
    def __init__(self):
        wide = lax.axis_index("wide")
        narrow = lax.axis_index("narrow")
        self.z = lax.rem(wide, Z)
        self.y = lax.rem(wide // Z, Y)
        self.x_lo = wide // (Y * Z)
        self.x_hi = narrow // 2
        self.core = lax.rem(narrow, 2)
        self.n = narrow
        self.x = self.x_hi * 2 + self.x_lo
        self.g = self.x * 2 + self.core

    def dev(self, x_hi=None, x_lo=None, core=None, y=None, z=None):
        x_hi = self.x_hi if x_hi is None else x_hi
        x_lo = self.x_lo if x_lo is None else x_lo
        core = self.core if core is None else core
        y = self.y if y is None else y
        z = self.z if z is None else z
        return ((x_lo * Y + y) * Z + z, x_hi * 2 + core)

    def in_group(self, g):
        return self.dev(x_hi=g // 4, x_lo=lax.rem(g // 2, 2), core=lax.rem(g, 2))


def step(value, by, size):
    return lax.rem(value + (by % size), size)


def greet(devices):
    barrier = pltpu.get_barrier_semaphore()
    for device in devices:
        pl.semaphore_signal(barrier, inc=1, device_id=device, device_id_type=MESH)
    return lambda: pl.semaphore_wait(barrier, len(devices))


class Net:
    def __init__(self, me, send_sems, recv_sems):
        self.me = me
        self.send_sems = send_sems
        self.recv_sems = recv_sems
        self.sent = 0
        self.keys = {}
        self.pending = []

    def sem(self, key):
        return self.recv_sems.at[self.keys.setdefault(key, len(self.keys))]

    def send(self, src, dst, to, key, when=None):
        copy = pltpu.make_async_remote_copy(
            src_ref=src, dst_ref=dst, send_sem=self.send_sems.at[self.sent],
            recv_sem=self.sem(key), device_id=to, device_id_type=MESH,
        )
        self.sent += 1
        if when is None:
            copy.start()
        else:
            pl.when(when)(copy.start)
        self.pending.append((when, copy))
        return copy

    def arrive(self, dst, key, when=None):
        copy = pltpu.make_async_remote_copy(
            src_ref=dst, dst_ref=dst, send_sem=self.send_sems.at[0], recv_sem=self.sem(key),
            device_id=self.me.dev(core=1 - self.me.core), device_id_type=MESH,
        )
        if when is None:
            copy.wait_recv()
        else:
            pl.when(when)(copy.wait_recv)

    def finish(self):
        for when, copy in self.pending:
            if when is None:
                copy.wait_send()
            else:
                pl.when(when)(copy.wait_send)


def ups(size, odd):
    return size // 2 if odd == 0 else size - 1 - size // 2


class Gather:
    def __init__(self, net, name, buf, slot, relative=False):
        self.net, self.name, self.buf, self.slot, self.relative = net, name, buf, slot, relative

    def send(self, axis, back_y, back_z, way):
        net, me = self.net, self.net.me
        src = self.buf.at[self.slot(back_y, back_z)]
        if axis == "y":
            key = (self.name, (back_y + way) % Y, back_z % Z)
            net.send(src, src, me.dev(y=step(me.y, way, Y)), key)
        else:
            dst = self.buf.at[self.slot(back_y, back_z + way)] if self.relative else src
            key = (self.name, back_y % Y, (back_z + way) % Z)
            net.send(src, dst, me.dev(z=step(me.z, way, Z)), key)

    def arrive(self, back_y, back_z):
        key = (self.name, back_y % Y, back_z % Z)
        self.net.arrive(self.buf.at[self.slot(back_y, back_z)], key)

    def ring(self, axis, fixed, far, odd):
        size = Y if axis == "y" else Z
        up = ups(size, odd % 2)
        for way, reach in ((1, up), (-1, size - 1 - up)):
            if far > reach:
                continue
            at = (far * way, fixed) if axis == "y" else (fixed, far * way)
            if far > 0:
                self.arrive(*at)
            if far < reach:
                self.send(axis, *at, way)

    def direct_y(self):
        for back in range(1, Y):
            self.send("y", 0, 0, back)


class PairShare:
    def __init__(self, net, name, src, dst, parts):
        self.net, self.name, self.src, self.dst = net, name, src, dst
        self.half = src.shape[0] // 2
        self.width = src.shape[1] // parts
        self.parts = parts
        me = net.me
        self.home = me.x_lo == me.core
        self.away = me.x_lo != me.core
        self.relayed = []

    def rows(self, which):
        return pl.ds(which * self.half, self.half)

    def columns(self, part):
        return slice(part * self.width, part * self.width + self.width)

    def start(self, part):
        me, net = self.net.me, self.net
        columns = self.columns(part)
        for core in range(2):
            net.send(
                self.src.at[self.rows(core), columns],
                self.dst.at[me.x_lo, self.rows(core), columns],
                me.dev(x_lo=1 - me.x_lo, core=core), (self.name, part, 0), when=self.away,
            )
        net.send(
            self.src.at[:, columns], self.dst.at[me.x_lo, :, columns],
            me.dev(core=1 - me.core), (self.name, part, 1), when=self.home,
        )

    def relay(self, part):
        me, net = self.net.me, self.net
        block = self.dst.at[1 - me.x_lo, self.rows(me.core), self.columns(part)]
        net.arrive(block, (self.name, part, 0))
        self.relayed.append(net.send(block, block, me.dev(core=1 - me.core), (self.name, part, 2)))
        net.pending.pop()

    def end(self):
        me, net = self.net.me, self.net
        for part in range(self.parts):
            columns = self.columns(part)
            other = self.dst.at[1 - me.x_lo, self.rows(1 - me.core), columns]
            net.arrive(other, (self.name, part, 2))
            whole = self.dst.at[me.x_lo, :, columns]
            net.arrive(whole, (self.name, part, 1), when=self.away)
        for copy in self.relayed:
            copy.wait_send()


def position(back_z):
    back_z = back_z % Z
    return 2 * back_z - (back_z > 0) if back_z <= Z // 2 else 2 * (Z - back_z)


def nt(a, b):
    return lax.dot_general(a, b, (((1,), (1,)), ((), ())), preferred_element_type=jnp.float32)


def tn_t(a, b):
    return lax.dot_general(a, b, (((0,), (1,)), ((), ())), preferred_element_type=jnp.float32)


def spread_group(net, name, buf):
    mine = buf.at[net.me.g]
    for back in range(1, GROUP):
        net.send(mine, mine, net.me.in_group(step(net.me.g, back, GROUP)), (name, back))


def collect_group(net, name, buf):
    for back in range(1, GROUP):
        net.arrive(buf.at[step(net.me.g, -back, GROUP)], (name, back))


def spread_y(net, name, buf):
    mine = buf.at[net.me.y]
    for back in range(1, Y):
        net.send(mine, mine, net.me.dev(y=step(net.me.y, back, Y)), (name, back))


def collect_y(net, name, buf):
    for back in range(1, Y):
        net.arrive(buf.at[step(net.me.y, -back, Y)], (name, back))


def spread_z(net, name, buf):
    mine = buf.at[net.me.z]
    for back in range(1, Z):
        net.send(mine, mine, net.me.dev(z=step(net.me.z, back, Z)), (name, back))


def collect_z(net, name, buf):
    for back in range(1, Z):
        net.arrive(buf.at[step(net.me.z, -back, Z)], (name, back))


def rotate_kernel(
    train, basis, eigs, train_out, small, query_in, query_out,
    out_side, qr, eig_sum, part_sum,
    tr, sides, eigs_all, eigs_round, inverse, outer_own, outer,
    scaled, ts, pairs, f1, f2, f3,
    train_all, basis_all, outer_all, small_all, small_pad,
    basis_own, query_rows, query_cols, eigs_own,
    cpart, c_in, st, s_in, sq, sq_in, qp, qp_in, e1, e2, e3,
    send_sems, recv_sems, local_sems,
):
    bf16, f32 = jnp.bfloat16, jnp.float32
    me = Place()
    net = Net(me, send_sems, recv_sems)
    home = me.x_lo == me.core
    away = me.x_lo != me.core
    swapped = dict(x_lo=me.core, core=me.x_lo)

    loads = [
        pltpu.make_async_copy(train_out, outer_own, local_sems.at[8 + 2 * Y]),
        pltpu.make_async_copy(eigs, eigs_own, local_sems.at[5]),
        pltpu.make_async_copy(basis, basis_own, local_sems.at[6]),
        pltpu.make_async_copy(query_in, query_rows, local_sems.at[7]),
    ]
    cols_z = me.z // 2 * 128
    for part in range(2 * Y):
        offset = pl.multiple_of(part * (query_out.shape[1] // (2 * Y)) + cols_z, 128)
        loads.append(
            pltpu.make_async_copy(
                query_out.at[:, pl.ds(offset, 128)],
                query_cols.at[:, part * 128 : part * 128 + 128],
                local_sems.at[8 + part],
            )
        )
    for load in loads:
        load.start()
    partners = []
    for back in range(Y):
        for flip_x in range(2):
            for flip_core in range(2):
                if back + flip_x + flip_core > 0:
                    partners.append(
                        me.dev(
                            x_lo=1 - me.x_lo if flip_x else me.x_lo,
                            core=1 - me.core if flip_core else me.core,
                            y=step(me.y, back, Y),
                        )
                    )
    for back in range(1, Z):
        partners.append(me.dev(z=step(me.z, back, Z), **swapped))
        partners.append(me.dev(z=step(me.z, back, Z)))
    for x_lo in range(2):
        for core in range(2):
            partners.append(me.dev(x_hi=1 - me.x_hi, x_lo=x_lo, core=core))
    all_here = greet(partners)
    small_pad[...] = jnp.zeros_like(small_pad)
    loads[0].wait()
    depth = small.shape[0]
    for z in range(Z):
        pieces = []
        for part in range(2 * Y):
            first = (part * Z + z) * depth
            pieces.append(outer_own[:, first : first + depth])
        outer[z] = jnp.concatenate(pieces, axis=1)
    all_here()

    own_slot = train_all.at[0, me.y]
    own_copy = pltpu.make_async_copy(train, own_slot, local_sems.at[0])
    pl.when(home)(own_copy.start)
    net.send(train, own_slot, me.dev(**swapped), "swap", when=away)

    outer_slot = outer_all.at[me.z, me.y]
    outer_copy = pltpu.make_async_copy(outer.at[me.z], outer_slot, local_sems.at[1])
    pl.when(home)(outer_copy.start)
    net.send(outer.at[me.z], outer_slot, me.dev(**swapped), ("outer", 0), when=away)
    for back in range(1, Z):
        to_z = step(me.z, back, Z)
        net.send(outer.at[to_z], outer_slot, me.dev(z=to_z, **swapped), ("outer", back))

    width = small.shape[1] // Y
    small_slot = me.x_lo * Y + me.y

    def small_part(y):
        return small.at[:, pl.ds(pl.multiple_of(y * width, width), width)]

    small_copy = pltpu.make_async_copy(small_part(me.y), small_all.at[small_slot], local_sems.at[2])
    pl.when(home)(small_copy.start)
    for back in range(Y):
        to_y = step(me.y, back, Y)
        for core in range(2):
            pair = net.keys.setdefault(("small", back, 0), len(net.keys))
            other = net.keys.setdefault(("small", back, 1), len(net.keys))
            copy = pltpu.make_async_remote_copy(
                src_ref=small_part(to_y), dst_ref=small_all.at[small_slot],
                send_sem=net.send_sems.at[net.sent],
                recv_sem=net.recv_sems.at[pair + (other - pair) * me.x_lo],
                device_id=me.dev(x_lo=me.core, core=core, y=to_y), device_id_type=MESH,
            )
            net.sent += 1
            when = None
            if back == 0:
                when = jnp.logical_or(away, me.core != core)
                pl.when(when)(copy.start)
            else:
                copy.start()
            net.pending.append((when, copy))

    rows_q = qp.shape[0] // 4
    loads[1].wait()
    tile = jnp.sum(eigs_own[...].reshape(-1, 8, eigs_own.shape[1]), axis=0)
    e1[me.g] = sum(tile[:, 128 * part : 128 * part + 128] for part in range(tile.shape[1] // 128))
    spread_group(net, "e1", e1)
    eigs_round[...] = eigs_own[...].astype(bf16)

    pl.when(home)(own_copy.wait)
    net.arrive(own_slot, "swap", when=away)
    cut = train.shape[1] // 896 * 128

    def spread(name, columns):
        return Gather(
            net, name, train_all,
            lambda back_y, back_z: (
                position(back_z), step(me.y, -back_y, Y), slice(None), columns
            ),
            relative=True,
        )

    lows = spread("low", slice(0, cut))
    trains = spread("train", slice(cut, train.shape[1]))

    def groups(far):
        return (far,) if far in (0, Z // 2) else (far, -far)

    def train_z(far):
        trains.ring("z", 0, far, 0)
        for back_z in groups(far):
            trains.ring("y", back_z, 0, back_z)
        if far > 0:
            for back in range(Y):
                lows.ring("z", back, far, back)

    def train_y(far):
        for hop in range(1, Y // 2 + 1):
            for back_z in groups(far):
                trains.ring("y", back_z, hop, back_z)

    def side_z(far):
        for back in range(Y):
            smalls.ring("z", back, far, back)

    lows.direct_y()
    train_z(0)
    lows.ring("z", 0, 0, 0)
    share_basis = PairShare(net, "basis", basis, basis_all, 4)
    share_eigs = PairShare(net, "eigs", eigs_round, eigs_all, 1)

    def outer_rows():
        pl.when(home)(outer_copy.wait)
        net.arrive(outer_slot, ("outer", 0), when=away)
        for back in range(1, Z):
            net.arrive(outer_all.at[step(me.z, -back, Z), me.y], ("outer", back))
        block = outer_all.at[:, me.y]
        for back in range(1, Y):
            net.send(block, block, me.dev(y=step(me.y, back, Y)), ("outer_y", back))

    def query_parts():
        loads[2].wait()
        loads[3].wait()
        qp[...] = nt(basis_own[...], query_rows[...])
        for back in range(1, 4):
            to_n = step(me.n, back, 4)
            net.send(
                qp.at[pl.ds(to_n * rows_q, rows_q)], qp_in.at[back],
                me.dev(x_hi=to_n // 2, core=lax.rem(to_n, 2)), ("qp", back),
            )

    def place_own():
        @pl.when(home)
        def _():
            basis_all[me.x_lo] = basis_own[...]
            eigs_all[me.x_lo] = eigs_round[...]

    rows_s = st.shape[0] // Z
    cols = st.shape[1]

    def side_parts():
        pl.when(home)(small_copy.wait)
        for x_lo in range(2):
            for back in range(Y):
                slot = small_all.at[x_lo * Y + step(me.y, -back, Y)]
                if back == 0:
                    here = jnp.logical_and(home, me.x_lo == x_lo)
                    net.arrive(slot, ("small", back, x_lo), when=jnp.logical_not(here))
                else:
                    net.arrive(slot, ("small", back, x_lo))
        for load in loads[4:]:
            load.wait()
        pad_row = lax.rem(me.z, 2) * depth
        for part in range(2 * Y):
            at = pl.ds(pl.multiple_of(part * 128 + pad_row, depth), depth)
            small_pad[at, :] = small_all[part]
        sq[...] = tn_t(small_pad[...], query_cols[...])
        for back in range(1, Z):
            to_z = step(me.z, back, Z)
            part = pl.ds(pl.multiple_of(to_z * rows_s, rows_s), rows_s)
            net.send(sq.at[part], sq_in.at[back], me.dev(z=to_z), ("side_q", back))
        for back in range(1, Y):
            net.arrive(outer_all.at[:, step(me.y, -back, Y)], ("outer_y", back))
        st[...] = tn_t(
            small_all[...].reshape(-1, width), outer_all[...].reshape(-1, 2 * Y * depth)
        ).astype(bf16)
        for back in range(1, Z):
            to_z = step(me.z, back, Z)
            part = pl.ds(pl.multiple_of(to_z * rows_s, rows_s), rows_s)
            net.send(st.at[part], s_in.at[back], me.dev(z=to_z), ("side", back))

    def query_sums():
        part = pl.ds(me.n * rows_q, rows_q)
        total = qp[part]
        for back in range(1, 4):
            net.arrive(qp_in.at[back], ("qp", back))
            total += qp_in[back]
        qr[me.x_lo, part] = total
        mine = qr.at[me.x_lo, part]
        for back in range(1, GROUP):
            net.send(mine, mine, me.in_group(step(me.g, back, GROUP)), ("qr", back))

    def side_sums():
        part = pl.ds(pl.multiple_of(me.z * rows_s, rows_s), rows_s)
        total = st[part].astype(f32)
        total_q = sq[part]
        for back in range(1, Z):
            net.arrive(sq_in.at[back], ("side_q", back))
            total_q += sq_in[back]
            net.arrive(s_in.at[back], ("side", back))
            total += s_in[back].astype(f32)
        sides[me.y, me.z, :, :cols] = total.astype(bf16)
        sides[me.y, me.z, :, cols:] = total_q.astype(bf16)

    smalls = Gather(
        net, "sides", sides,
        lambda back_y, back_z: (step(me.y, -back_y, Y), step(me.z, -back_z, Z)),
    )
    rows_c = cpart.shape[0] // X
    rows_g = Y * train.shape[0]

    def lanes(batch):
        low, high = (0, 1) if batch == 0 else (2 * batch - 1, min(2 * batch + 1, Z))
        return low, high, slice(low * rows_g, high * rows_g)

    def x_part(x):
        return pl.ds(pl.multiple_of(x * rows_c, rows_c), rows_c)

    def to_x(back):
        x = step(me.x, back, X)
        return x, me.dev(x_hi=x // 2, x_lo=lax.rem(x, 2))

    def multiply(batch):
        low, high, span = lanes(batch)
        rows = train_all[low:high].reshape((high - low) * rows_g, train.shape[1])
        both = basis_all[...].reshape(-1, train.shape[1])
        cpart[:, span] = nt(both, rows).astype(bf16)
        for back in range(1, X):
            x, device = to_x(back)
            net.send(
                cpart.at[x_part(x), span], c_in.at[back, :, span], device, ("ct", batch, back)
            )

    def combine(batch):
        span = lanes(batch)[2]
        part = x_part(me.x)
        total = cpart[part, span].astype(f32)
        for back in range(1, X):
            net.arrive(c_in.at[back, :, span], ("ct", batch, back))
            total += c_in[back, :, span].astype(f32)
        tr[part, span] = total.astype(bf16)
        mine = tr.at[part, span]
        for back in range(1, X):
            net.send(mine, mine, to_x(back)[1], ("tr", batch, back))

    def swap_queries(far):
        for back_z in groups(far):
            z = step(me.z, -back_z, Z)
            net.send(
                sides.at[:, z, :, cols:], out_side.at[:, z], me.dev(**swapped),
                ("swap_q", back_z % Z), when=away,
            )

    def score(batches):
        for batch in batches:
            for back in range(1, X):
                part = x_part(step(me.x, -back, X))
                net.arrive(tr.at[part, lanes(batch)[2]], ("tr", batch, back))
        span = slice(lanes(batches[0])[2].start, lanes(batches[-1])[2].stop)

        def one(query, carry):
            projected = jnp.dot(scaled[query], ts[:, span], preferred_element_type=f32)
            product = projected * tr[:, span].astype(f32)
            pairs[query, :, span] = jnp.sum(product.reshape(-1, 8, product.shape[1]), axis=0)
            return carry

        lax.fori_loop(0, pairs.shape[0], one, 0, unroll=2)

    def pick(block, query):
        lane = lax.broadcasted_iota(jnp.int32, block.shape, 1)
        keep = jnp.logical_and(lane >= query * RANK, lane < (query + 1) * RANK)
        return jnp.where(keep, block, 0.0).astype(bf16)

    def scale(query, carry):
        left = pick(qr[...].reshape(-1, qr.shape[2]), query)
        product = nt(left, sides[:, :, :, cols:].reshape(-1, qr.shape[2]))
        scaled[query] = (product * inverse[...].reshape(product.shape)).astype(bf16)
        return carry

    outer_rows()
    share_basis.start(0)
    for back in range(1, Y):
        lows.arrive(back, 0)
        lows.ring("z", back, 0, back)
    train_z(1)
    query_parts()
    side_parts()
    train_z(2)
    share_basis.start(1)
    query_sums()
    collect_group(net, "e1", e1)
    e2[me.y] = jnp.sum(e1[...], axis=0)
    spread_y(net, "e2", e2)
    train_z(3)
    share_basis.start(2)
    share_basis.start(3)
    share_eigs.start(0)
    side_sums()
    smalls.direct_y()
    smalls.ring("z", 0, 0, 0)
    train_y(0)
    train_z(4)
    place_own()
    for back in range(1, Y):
        smalls.arrive(back, 0)
        smalls.ring("z", back, 0, back)
    swap_queries(0)
    train_y(1)
    side_z(1)
    swap_queries(1)
    share_basis.relay(0)
    share_basis.relay(1)
    collect_y(net, "e2", e2)
    e3[me.z] = jnp.sum(e2[...], axis=0)
    spread_z(net, "e3", e3)
    side_z(2)
    swap_queries(2)
    share_basis.relay(2)
    share_basis.relay(3)
    share_eigs.relay(0)
    train_y(2)
    side_z(3)
    swap_queries(3)
    share_basis.end()
    multiply(0)
    multiply(1)
    side_z(4)
    swap_queries(4)
    multiply(2)
    combine(0)
    collect_z(net, "e3", e3)
    eig_sum[...] = jnp.sum(e3[...], axis=0)
    damp = (0.1 / (DS * DA)) * jnp.sum(eig_sum[...])
    for back in range(1, GROUP):
        g = step(me.g, -back, GROUP)
        n = (g // 4) * 2 + lax.rem(g, 2)
        net.arrive(qr.at[lax.rem(g // 2, 2), pl.ds(n * rows_q, rows_q)], ("qr", back))
    share_eigs.end()
    inverse[...] = 1.0 / (eigs_all[...].astype(f32) + damp)
    combine(1)
    train_y(3)
    multiply(3)
    queries = pairs.shape[0]
    lax.fori_loop(0, queries, scale, 0, unroll=2)
    for back in range(Z):
        at = position(back) * rows_g
        start = pl.multiple_of(step(me.z, -back, Z) * rows_g, rows_g)
        ts[:, at : at + rows_g] = sides[:, :, :, pl.ds(start, rows_g)].reshape(-1, rows_g)
    combine(2)
    train_y(4)
    multiply(4)
    combine(3)
    score((0, 1, 2))
    combine(4)
    score((3, 4))

    rows = tr.shape[1]
    row = lax.broadcasted_iota(jnp.int32, (rows, 128), 0)
    lane = lax.broadcasted_iota(jnp.int32, (rows, 128), 1)
    place = row // rows_g
    back = jnp.where(place % 2 == 1, (place + 1) // 2, Z - place // 2)
    z = (me.z + Z - back) % Z
    sample = (me.core * Y + (row % rows_g) // RANK) * Z + z
    sums = jnp.dot(
        pairs[...].reshape(-1, rows), jnp.where(lane == sample, 1.0, 0.0),
        preferred_element_type=f32, precision=lax.Precision.HIGHEST,
    )
    f1[me.g] = jnp.sum(sums.reshape(-1, 8, 128), axis=1)
    spread_group(net, "f1", f1)

    collect_group(net, "f1", f1)
    f2[me.y] = jnp.sum(f1[...], axis=0)
    spread_y(net, "f2", f2)
    collect_y(net, "f2", f2)
    f3[me.z] = jnp.sum(f2[...], axis=0)
    spread_z(net, "f3", f3)
    for back_z in range(Z):
        net.arrive(out_side.at[:, step(me.z, -back_z, Z)], ("swap_q", back_z), when=away)

    @pl.when(home)
    def _():
        out_side[...] = sides[:, :, :, cols:]

    collect_z(net, "f3", f3)
    part_sum[...] = jnp.sum(f3[...], axis=0)
    net.finish()


def precond_kernel(out_side, qr, eig_sum, part_sum, eigs, precond, scores, inv):
    turn = pl.program_id(0)
    x_lo = Place().x_lo
    each = precond.shape[0]

    @pl.when(turn == 0)
    def _():
        damp = (0.1 / (DS * DA)) * jnp.sum(eig_sum[...])
        inv[...] = 1.0 / (eigs[...] + damp)
        total = part_sum[:, : scores.shape[1]]
        scores[...] = total / jnp.sqrt(jnp.float32(RANK * DS * DA))

    for sub in range(each):
        query = turn * each + sub
        block = qr[x_lo]
        lane = lax.broadcasted_iota(jnp.int32, block.shape, 1)
        keep = jnp.logical_and(lane >= query * RANK, lane < (query + 1) * RANK)
        left = jnp.where(keep, block, 0.0).astype(jnp.bfloat16)
        precond[sub] = (nt(left, out_side[...]) * inv[...]).astype(jnp.bfloat16)


def precondition(out_side, qr, eig_sum, part_sum, eigs):
    queries = part_sum.shape[0]
    each = 2
    return pl.pallas_call(
        precond_kernel,
        grid=(queries // each,),
        out_shape=(
            jax.ShapeDtypeStruct((queries,) + eigs.shape, jnp.bfloat16),
            jax.ShapeDtypeStruct((queries, 2 * Y * Z), jnp.float32),
        ),
        in_specs=[VMEM] * 5,
        out_specs=(
            pl.BlockSpec((each,) + eigs.shape, lambda q: (q, 0, 0)),
            pl.BlockSpec((queries, 2 * Y * Z), lambda q: (0, 0)),
        ),
        scratch_shapes=[pltpu.VMEM(eigs.shape, jnp.float32)],
        compiler_params=pltpu.CompilerParams(vmem_limit_bytes=12 << 20),
        name="precondition",
    )(out_side, qr, eig_sum, part_sum, eigs)


def influence(train, basis, eigs, train_out, small, query_in, query_out, queries):
    bf16, f32 = jnp.bfloat16, jnp.float32
    rank, coords = train.shape
    block = basis.shape[0]
    wide = small.shape[1]
    width = wide // Y
    rows = Y * Z * rank
    query_rows = query_in.shape[0]
    rows_s = width // Z
    outer = (Z, rank, train_out.shape[1] // Z)
    return pl.pallas_call(
        rotate_kernel,
        out_shape=(
            jax.ShapeDtypeStruct((Y, Z, rows_s, query_rows), bf16),
            jax.ShapeDtypeStruct((2, block, query_rows), f32),
            jax.ShapeDtypeStruct((8, 128), f32),
            jax.ShapeDtypeStruct((queries, 128), f32),
        ),
        in_specs=[ANY] * 7,
        out_specs=[VMEM] * 4,
        scratch_shapes=[
            pltpu.VMEM((2 * block, rows), bf16),
            pltpu.VMEM((Y, Z, rows_s, rows + query_rows), bf16),
            pltpu.VMEM((2,) + eigs.shape, bf16),
            pltpu.VMEM(eigs.shape, bf16),
            pltpu.VMEM((2,) + eigs.shape, f32),
            pltpu.VMEM(train_out.shape, bf16),
            pltpu.VMEM(outer, bf16),
            pltpu.VMEM((queries, 2 * block, wide), bf16),
            pltpu.VMEM((wide, rows), bf16),
            pltpu.VMEM((queries, 8, rows), f32),
            pltpu.VMEM((GROUP, 8, 128), f32),
            pltpu.VMEM((Y, 8, 128), f32),
            pltpu.VMEM((Z, 8, 128), f32),
            pltpu.VMEM((Z, Y, rank, coords), bf16),
            pltpu.VMEM((2, block, coords), bf16),
            pltpu.VMEM((Z, Y) + outer[1:], bf16),
            pltpu.VMEM((2 * Y, small.shape[0], width), bf16),
            pltpu.VMEM((2 * Y * 128, width), bf16),
            pltpu.VMEM(basis.shape, bf16),
            pltpu.VMEM(query_in.shape, bf16),
            pltpu.VMEM((query_rows, 2 * Y * 128), bf16),
            pltpu.VMEM(eigs.shape, f32),
            pltpu.VMEM((2 * block, rows), bf16),
            pltpu.VMEM((X, 2 * block // X, rows), bf16),
            pltpu.VMEM((width, rows), bf16),
            pltpu.VMEM((Z, rows_s, rows), bf16),
            pltpu.VMEM((width, query_rows), f32),
            pltpu.VMEM((Z, rows_s, query_rows), f32),
            pltpu.VMEM((block, query_rows), f32),
            pltpu.VMEM((4, block // 4, query_rows), f32),
            pltpu.VMEM((GROUP, 8, 128), f32),
            pltpu.VMEM((Y, 8, 128), f32),
            pltpu.VMEM((Z, 8, 128), f32),
            pltpu.SemaphoreType.DMA((288,)),
            pltpu.SemaphoreType.DMA((288,)),
            pltpu.SemaphoreType.DMA((9 + 2 * Y,)),
        ],
        compiler_params=pltpu.CompilerParams(
            collective_id=0, has_side_effects=True, vmem_limit_bytes=58 << 20
        ),
        name="influence",
    )(train, basis, eigs, train_out, small, query_in, query_out)


def shards(query_in, query_out, train_in, train_out, basis_in, basis_out, eigvals):
    queries, qrank, coords = query_in.shape
    eigs = eigvals.T
    out_side, qr, eig_sum, part_sum = influence(
        train_in[0], basis_in, eigs, train_out[0], basis_out.T,
        query_in.reshape(queries * qrank, coords),
        query_out.reshape(queries * qrank, query_out.shape[2]), queries,
    )
    precond, scores = precondition(
        out_side.reshape(-1, out_side.shape[3]), qr, eig_sum, part_sum, eigs
    )
    return precond.transpose(0, 2, 1), scores


def solution(mesh):
    placed = (
        P(None, None, "narrow"),
        P(),
        P("wide", None, "narrow"),
        P("wide", None, None),
        P("wide", "narrow"),
        P("narrow", "wide"),
        P("narrow", "wide"),
    )
    return jax.shard_map(
        shards,
        mesh=mesh,
        in_specs=placed,
        out_specs=(P(None, "narrow", "wide"), P()),
        check_vma=False,
    )
```

```python
import jax
import jax.numpy as jnp
from jax import lax
from jax.experimental import pallas as pl
from jax.experimental.pallas import tpu as pltpu
from jax.sharding import PartitionSpec as P

DS = 4096
DA = 14336
RANK = 32
Y = 4
Z = 8
X = 4
GROUP = 8
MESH = pl.DeviceIdType.MESH
VMEM = pl.BlockSpec(memory_space=pltpu.VMEM)
ANY = pl.BlockSpec(memory_space=pl.ANY)


class Place:
    def __init__(self):
        wide = lax.axis_index("wide")
        narrow = lax.axis_index("narrow")
        self.z = lax.rem(wide, Z)
        self.y = lax.rem(wide // Z, Y)
        self.x_lo = wide // (Y * Z)
        self.x_hi = narrow // 2
        self.core = lax.rem(narrow, 2)
        self.n = narrow
        self.x = self.x_hi * 2 + self.x_lo
        self.g = self.x * 2 + self.core

    def dev(self, x_hi=None, x_lo=None, core=None, y=None, z=None):
        x_hi = self.x_hi if x_hi is None else x_hi
        x_lo = self.x_lo if x_lo is None else x_lo
        core = self.core if core is None else core
        y = self.y if y is None else y
        z = self.z if z is None else z
        return ((x_lo * Y + y) * Z + z, x_hi * 2 + core)

    def in_group(self, g):
        return self.dev(x_hi=g // 4, x_lo=lax.rem(g // 2, 2), core=lax.rem(g, 2))


def step(value, by, size):
    return lax.rem(value + (by % size), size)


def greet(devices):
    barrier = pltpu.get_barrier_semaphore()
    for device in devices:
        pl.semaphore_signal(barrier, inc=1, device_id=device, device_id_type=MESH)
    return lambda: pl.semaphore_wait(barrier, len(devices))


class Net:
    def __init__(self, me, send_sems, recv_sems):
        self.me = me
        self.send_sems = send_sems
        self.recv_sems = recv_sems
        self.sent = 0
        self.keys = {}
        self.pending = []

    def sem(self, key):
        return self.recv_sems.at[self.keys.setdefault(key, len(self.keys))]

    def send(self, src, dst, to, key, when=None):
        copy = pltpu.make_async_remote_copy(
            src_ref=src, dst_ref=dst, send_sem=self.send_sems.at[self.sent],
            recv_sem=self.sem(key), device_id=to, device_id_type=MESH,
        )
        self.sent += 1
        if when is None:
            copy.start()
        else:
            pl.when(when)(copy.start)
        self.pending.append((when, copy))
        return copy

    def arrive(self, dst, key, when=None):
        copy = pltpu.make_async_remote_copy(
            src_ref=dst, dst_ref=dst, send_sem=self.send_sems.at[0], recv_sem=self.sem(key),
            device_id=self.me.dev(core=1 - self.me.core), device_id_type=MESH,
        )
        if when is None:
            copy.wait_recv()
        else:
            pl.when(when)(copy.wait_recv)

    def finish(self):
        for when, copy in self.pending:
            if when is None:
                copy.wait_send()
            else:
                pl.when(when)(copy.wait_send)


def ups(size, odd):
    return size // 2 if odd == 0 else size - 1 - size // 2


class Gather:
    def __init__(self, net, name, buf, slot, relative=False):
        self.net, self.name, self.buf, self.slot, self.relative = net, name, buf, slot, relative

    def send(self, axis, back_y, back_z, way):
        net, me = self.net, self.net.me
        src = self.buf.at[self.slot(back_y, back_z)]
        if axis == "y":
            key = (self.name, (back_y + way) % Y, back_z % Z)
            net.send(src, src, me.dev(y=step(me.y, way, Y)), key)
        else:
            dst = self.buf.at[self.slot(back_y, back_z + way)] if self.relative else src
            key = (self.name, back_y % Y, (back_z + way) % Z)
            net.send(src, dst, me.dev(z=step(me.z, way, Z)), key)

    def arrive(self, back_y, back_z):
        key = (self.name, back_y % Y, back_z % Z)
        self.net.arrive(self.buf.at[self.slot(back_y, back_z)], key)

    def ring(self, axis, fixed, far, odd):
        size = Y if axis == "y" else Z
        up = ups(size, odd % 2)
        for way, reach in ((1, up), (-1, size - 1 - up)):
            if far > reach:
                continue
            at = (far * way, fixed) if axis == "y" else (fixed, far * way)
            if far > 0:
                self.arrive(*at)
            if far < reach:
                self.send(axis, *at, way)

    def direct_y(self):
        for back in range(1, Y):
            self.send("y", 0, 0, back)


class PairShare:
    def __init__(self, net, name, src, dst, parts):
        self.net, self.name, self.src, self.dst = net, name, src, dst
        self.half = src.shape[0] // 2
        self.width = src.shape[1] // parts
        self.parts = parts
        me = net.me
        self.home = me.x_lo == me.core
        self.away = me.x_lo != me.core
        self.relayed = []

    def rows(self, which):
        return pl.ds(which * self.half, self.half)

    def columns(self, part):
        return slice(part * self.width, part * self.width + self.width)

    def start(self, part):
        me, net = self.net.me, self.net
        columns = self.columns(part)
        for core in range(2):
            net.send(
                self.src.at[self.rows(core), columns],
                self.dst.at[me.x_lo, self.rows(core), columns],
                me.dev(x_lo=1 - me.x_lo, core=core), (self.name, part, 0), when=self.away,
            )
        net.send(
            self.src.at[:, columns], self.dst.at[me.x_lo, :, columns],
            me.dev(core=1 - me.core), (self.name, part, 1), when=self.home,
        )

    def relay(self, part):
        me, net = self.net.me, self.net
        block = self.dst.at[1 - me.x_lo, self.rows(me.core), self.columns(part)]
        net.arrive(block, (self.name, part, 0))
        self.relayed.append(net.send(block, block, me.dev(core=1 - me.core), (self.name, part, 2)))
        net.pending.pop()

    def end(self):
        me, net = self.net.me, self.net
        for part in range(self.parts):
            columns = self.columns(part)
            other = self.dst.at[1 - me.x_lo, self.rows(1 - me.core), columns]
            net.arrive(other, (self.name, part, 2))
            whole = self.dst.at[me.x_lo, :, columns]
            net.arrive(whole, (self.name, part, 1), when=self.away)
        for copy in self.relayed:
            copy.wait_send()


def position(back_z):
    back_z = back_z % Z
    return 2 * back_z - (back_z > 0) if back_z <= Z // 2 else 2 * (Z - back_z)


def nt(a, b):
    return lax.dot_general(a, b, (((1,), (1,)), ((), ())), preferred_element_type=jnp.float32)


def tn_t(a, b):
    return lax.dot_general(a, b, (((0,), (1,)), ((), ())), preferred_element_type=jnp.float32)


def spread_group(net, name, buf):
    mine = buf.at[net.me.g]
    for back in range(1, GROUP):
        net.send(mine, mine, net.me.in_group(step(net.me.g, back, GROUP)), (name, back))


def collect_group(net, name, buf):
    for back in range(1, GROUP):
        net.arrive(buf.at[step(net.me.g, -back, GROUP)], (name, back))


def spread_y(net, name, buf):
    mine = buf.at[net.me.y]
    for back in range(1, Y):
        net.send(mine, mine, net.me.dev(y=step(net.me.y, back, Y)), (name, back))


def collect_y(net, name, buf):
    for back in range(1, Y):
        net.arrive(buf.at[step(net.me.y, -back, Y)], (name, back))


def spread_z(net, name, buf):
    mine = buf.at[net.me.z]
    for back in range(1, Z):
        net.send(mine, mine, net.me.dev(z=step(net.me.z, back, Z)), (name, back))


def collect_z(net, name, buf):
    for back in range(1, Z):
        net.arrive(buf.at[step(net.me.z, -back, Z)], (name, back))


def rotate_kernel(
    train, basis, eigs, train_out, small, query_in, query_out,
    out_side, qr, eig_sum, part_sum,
    tr, sides, eigs_all, eigs_round, inverse, outer_own, outer,
    scaled, ts, pairs, f1, f2, f3,
    train_all, basis_all, outer_all, small_all, small_pad,
    basis_own, query_rows, query_cols, eigs_own,
    cpart, c_in, st, s_in, sq, sq_in, qp, qp_in, e1, e2, e3,
    send_sems, recv_sems, local_sems,
):
    bf16, f32 = jnp.bfloat16, jnp.float32
    me = Place()
    net = Net(me, send_sems, recv_sems)
    home = me.x_lo == me.core
    away = me.x_lo != me.core
    swapped = dict(x_lo=me.core, core=me.x_lo)

    loads = [
        pltpu.make_async_copy(train_out, outer_own, local_sems.at[8 + 2 * Y]),
        pltpu.make_async_copy(eigs, eigs_own, local_sems.at[5]),
        pltpu.make_async_copy(basis, basis_own, local_sems.at[6]),
        pltpu.make_async_copy(query_in, query_rows, local_sems.at[7]),
    ]
    cols_z = me.z // 2 * 128
    for part in range(2 * Y):
        offset = pl.multiple_of(part * (query_out.shape[1] // (2 * Y)) + cols_z, 128)
        loads.append(
            pltpu.make_async_copy(
                query_out.at[:, pl.ds(offset, 128)],
                query_cols.at[:, part * 128 : part * 128 + 128],
                local_sems.at[8 + part],
            )
        )
    for load in loads:
        load.start()
    partners = []
    for back in range(Y):
        for flip_x in range(2):
            for flip_core in range(2):
                if back + flip_x + flip_core > 0:
                    partners.append(
                        me.dev(
                            x_lo=1 - me.x_lo if flip_x else me.x_lo,
                            core=1 - me.core if flip_core else me.core,
                            y=step(me.y, back, Y),
                        )
                    )
    for back in range(1, Z):
        partners.append(me.dev(z=step(me.z, back, Z), **swapped))
        partners.append(me.dev(z=step(me.z, back, Z)))
    for x_lo in range(2):
        for core in range(2):
            partners.append(me.dev(x_hi=1 - me.x_hi, x_lo=x_lo, core=core))
    all_here = greet(partners)
    small_pad[...] = jnp.zeros_like(small_pad)
    loads[0].wait()
    depth = small.shape[0]
    for z in range(Z):
        pieces = []
        for part in range(2 * Y):
            first = (part * Z + z) * depth
            pieces.append(outer_own[:, first : first + depth])
        outer[z] = jnp.concatenate(pieces, axis=1)
    all_here()

    own_slot = train_all.at[0, me.y]
    own_copy = pltpu.make_async_copy(train, own_slot, local_sems.at[0])
    pl.when(home)(own_copy.start)
    net.send(train, own_slot, me.dev(**swapped), "swap", when=away)

    outer_slot = outer_all.at[me.z, me.y]
    outer_copy = pltpu.make_async_copy(outer.at[me.z], outer_slot, local_sems.at[1])
    pl.when(home)(outer_copy.start)
    net.send(outer.at[me.z], outer_slot, me.dev(**swapped), ("outer", 0), when=away)
    for back in range(1, Z):
        to_z = step(me.z, back, Z)
        net.send(outer.at[to_z], outer_slot, me.dev(z=to_z, **swapped), ("outer", back))

    width = small.shape[1] // Y
    small_slot = me.x_lo * Y + me.y

    def small_part(y):
        return small.at[:, pl.ds(pl.multiple_of(y * width, width), width)]

    small_copy = pltpu.make_async_copy(small_part(me.y), small_all.at[small_slot], local_sems.at[2])
    pl.when(home)(small_copy.start)
    for back in range(Y):
        to_y = step(me.y, back, Y)
        for core in range(2):
            pair = net.keys.setdefault(("small", back, 0), len(net.keys))
            other = net.keys.setdefault(("small", back, 1), len(net.keys))
            copy = pltpu.make_async_remote_copy(
                src_ref=small_part(to_y), dst_ref=small_all.at[small_slot],
                send_sem=net.send_sems.at[net.sent],
                recv_sem=net.recv_sems.at[pair + (other - pair) * me.x_lo],
                device_id=me.dev(x_lo=me.core, core=core, y=to_y), device_id_type=MESH,
            )
            net.sent += 1
            when = None
            if back == 0:
                when = jnp.logical_or(away, me.core != core)
                pl.when(when)(copy.start)
            else:
                copy.start()
            net.pending.append((when, copy))

    rows_q = qp.shape[0] // 4
    loads[1].wait()
    tile = jnp.sum(eigs_own[...].reshape(-1, 8, eigs_own.shape[1]), axis=0)
    e1[me.g] = sum(tile[:, 128 * part : 128 * part + 128] for part in range(tile.shape[1] // 128))
    spread_group(net, "e1", e1)
    eigs_round[...] = eigs_own[...].astype(bf16)

    pl.when(home)(own_copy.wait)
    net.arrive(own_slot, "swap", when=away)
    cut = train.shape[1] // 896 * 256

    def spread(name, columns):
        return Gather(
            net, name, train_all,
            lambda back_y, back_z: (
                position(back_z), step(me.y, -back_y, Y), slice(None), columns
            ),
            relative=True,
        )

    lows = spread("low", slice(0, cut))
    trains = spread("train", slice(cut, train.shape[1]))

    def groups(far):
        return (far,) if far in (0, Z // 2) else (far, -far)

    def train_z(far):
        trains.ring("z", 0, far, 0)
        for back_z in groups(far):
            for back in range(1, Y):
                trains.send("y", 0, back_z, back)
        if far > 0:
            for back in range(Y):
                lows.ring("z", back, far, back)

    def train_y(far):
        for back_z in groups(far):
            for back in range(1, Y):
                trains.arrive(back, back_z)

    def side_z(far):
        for back in range(Y):
            smalls.ring("z", back, far, back)

    lows.direct_y()
    train_z(0)
    lows.ring("z", 0, 0, 0)
    share_basis = PairShare(net, "basis", basis, basis_all, 4)
    share_eigs = PairShare(net, "eigs", eigs_round, eigs_all, 1)

    def outer_rows():
        pl.when(home)(outer_copy.wait)
        net.arrive(outer_slot, ("outer", 0), when=away)
        for back in range(1, Z):
            net.arrive(outer_all.at[step(me.z, -back, Z), me.y], ("outer", back))
        block = outer_all.at[:, me.y]
        for back in range(1, Y):
            net.send(block, block, me.dev(y=step(me.y, back, Y)), ("outer_y", back))

    def query_parts():
        loads[2].wait()
        loads[3].wait()
        qp[...] = nt(basis_own[...], query_rows[...])
        for back in range(1, 4):
            to_n = step(me.n, back, 4)
            net.send(
                qp.at[pl.ds(to_n * rows_q, rows_q)], qp_in.at[back],
                me.dev(x_hi=to_n // 2, core=lax.rem(to_n, 2)), ("qp", back),
            )

    def place_own():
        @pl.when(home)
        def _():
            basis_all[me.x_lo] = basis_own[...]
            eigs_all[me.x_lo] = eigs_round[...]

    rows_s = st.shape[0] // Z
    cols = st.shape[1]

    def side_parts():
        pl.when(home)(small_copy.wait)
        for x_lo in range(2):
            for back in range(Y):
                slot = small_all.at[x_lo * Y + step(me.y, -back, Y)]
                if back == 0:
                    here = jnp.logical_and(home, me.x_lo == x_lo)
                    net.arrive(slot, ("small", back, x_lo), when=jnp.logical_not(here))
                else:
                    net.arrive(slot, ("small", back, x_lo))
        for load in loads[4:]:
            load.wait()
        pad_row = lax.rem(me.z, 2) * depth
        for part in range(2 * Y):
            at = pl.ds(pl.multiple_of(part * 128 + pad_row, depth), depth)
            small_pad[at, :] = small_all[part]
        sq[...] = tn_t(small_pad[...], query_cols[...])
        for back in range(1, Z):
            to_z = step(me.z, back, Z)
            part = pl.ds(pl.multiple_of(to_z * rows_s, rows_s), rows_s)
            net.send(sq.at[part], sq_in.at[back], me.dev(z=to_z), ("side_q", back))
        for back in range(1, Y):
            net.arrive(outer_all.at[:, step(me.y, -back, Y)], ("outer_y", back))
        st[...] = tn_t(
            small_all[...].reshape(-1, width), outer_all[...].reshape(-1, 2 * Y * depth)
        ).astype(bf16)
        for back in range(1, Z):
            to_z = step(me.z, back, Z)
            part = pl.ds(pl.multiple_of(to_z * rows_s, rows_s), rows_s)
            net.send(st.at[part], s_in.at[back], me.dev(z=to_z), ("side", back))

    def query_sums():
        part = pl.ds(me.n * rows_q, rows_q)
        total = qp[part]
        for back in range(1, 4):
            net.arrive(qp_in.at[back], ("qp", back))
            total += qp_in[back]
        qr[me.x_lo, part] = total
        mine = qr.at[me.x_lo, part]
        for back in range(1, GROUP):
            net.send(mine, mine, me.in_group(step(me.g, back, GROUP)), ("qr", back))

    def side_sums():
        part = pl.ds(pl.multiple_of(me.z * rows_s, rows_s), rows_s)
        total = st[part].astype(f32)
        total_q = sq[part]
        for back in range(1, Z):
            net.arrive(sq_in.at[back], ("side_q", back))
            total_q += sq_in[back]
            net.arrive(s_in.at[back], ("side", back))
            total += s_in[back].astype(f32)
        sides[me.y, me.z, :, :cols] = total.astype(bf16)
        sides[me.y, me.z, :, cols:] = total_q.astype(bf16)

    smalls = Gather(
        net, "sides", sides,
        lambda back_y, back_z: (step(me.y, -back_y, Y), step(me.z, -back_z, Z)),
    )
    rows_c = cpart.shape[0] // X
    rows_g = Y * train.shape[0]

    def lanes(batch):
        low, high = (0, 1) if batch == 0 else (2 * batch - 1, min(2 * batch + 1, Z))
        return low, high, slice(low * rows_g, high * rows_g)

    def x_part(x):
        return pl.ds(pl.multiple_of(x * rows_c, rows_c), rows_c)

    def to_x(back):
        x = step(me.x, back, X)
        return x, me.dev(x_hi=x // 2, x_lo=lax.rem(x, 2))

    def multiply(batch):
        low, high, span = lanes(batch)
        rows = train_all[low:high].reshape((high - low) * rows_g, train.shape[1])
        both = basis_all[...].reshape(-1, train.shape[1])
        cpart[:, span] = nt(both, rows).astype(bf16)
        for back in range(1, X):
            x, device = to_x(back)
            net.send(
                cpart.at[x_part(x), span], c_in.at[back, :, span], device, ("ct", batch, back)
            )

    def combine(batch):
        span = lanes(batch)[2]
        part = x_part(me.x)
        total = cpart[part, span].astype(f32)
        for back in range(1, X):
            net.arrive(c_in.at[back, :, span], ("ct", batch, back))
            total += c_in[back, :, span].astype(f32)
        tr[part, span] = total.astype(bf16)
        mine = tr.at[part, span]
        for back in range(1, X):
            net.send(mine, mine, to_x(back)[1], ("tr", batch, back))

    def swap_queries(far):
        for back_z in groups(far):
            z = step(me.z, -back_z, Z)
            net.send(
                sides.at[:, z, :, cols:], out_side.at[:, z], me.dev(**swapped),
                ("swap_q", back_z % Z), when=away,
            )

    def score(batches):
        for batch in batches:
            for back in range(1, X):
                part = x_part(step(me.x, -back, X))
                net.arrive(tr.at[part, lanes(batch)[2]], ("tr", batch, back))
        span = slice(lanes(batches[0])[2].start, lanes(batches[-1])[2].stop)

        def one(query, carry):
            projected = jnp.dot(scaled[query], ts[:, span], preferred_element_type=f32)
            product = projected * tr[:, span].astype(f32)
            pairs[query, :, span] = jnp.sum(product.reshape(-1, 8, product.shape[1]), axis=0)
            return carry

        lax.fori_loop(0, pairs.shape[0], one, 0, unroll=2)

    def pick(block, query):
        lane = lax.broadcasted_iota(jnp.int32, block.shape, 1)
        keep = jnp.logical_and(lane >= query * RANK, lane < (query + 1) * RANK)
        return jnp.where(keep, block, 0.0).astype(bf16)

    def scale(query, carry):
        left = pick(qr[...].reshape(-1, qr.shape[2]), query)
        product = nt(left, sides[:, :, :, cols:].reshape(-1, qr.shape[2]))
        scaled[query] = (product * inverse[...].reshape(product.shape)).astype(bf16)
        return carry

    outer_rows()
    share_basis.start(0)
    for back in range(1, Y):
        lows.arrive(back, 0)
        lows.ring("z", back, 0, back)
    train_z(1)
    query_parts()
    side_parts()
    train_z(2)
    share_basis.start(1)
    query_sums()
    collect_group(net, "e1", e1)
    e2[me.y] = jnp.sum(e1[...], axis=0)
    spread_y(net, "e2", e2)
    train_z(3)
    share_basis.start(2)
    share_basis.start(3)
    share_eigs.start(0)
    side_sums()
    smalls.direct_y()
    smalls.ring("z", 0, 0, 0)
    train_y(0)
    train_z(4)
    place_own()
    for back in range(1, Y):
        smalls.arrive(back, 0)
        smalls.ring("z", back, 0, back)
    swap_queries(0)
    train_y(1)
    side_z(1)
    swap_queries(1)
    share_basis.relay(0)
    share_basis.relay(1)
    collect_y(net, "e2", e2)
    e3[me.z] = jnp.sum(e2[...], axis=0)
    spread_z(net, "e3", e3)
    side_z(2)
    swap_queries(2)
    share_basis.relay(2)
    share_basis.relay(3)
    share_eigs.relay(0)
    train_y(2)
    side_z(3)
    swap_queries(3)
    share_basis.end()
    multiply(0)
    multiply(1)
    side_z(4)
    swap_queries(4)
    multiply(2)
    combine(0)
    collect_z(net, "e3", e3)
    eig_sum[...] = jnp.sum(e3[...], axis=0)
    damp = (0.1 / (DS * DA)) * jnp.sum(eig_sum[...])
    for back in range(1, GROUP):
        g = step(me.g, -back, GROUP)
        n = (g // 4) * 2 + lax.rem(g, 2)
        net.arrive(qr.at[lax.rem(g // 2, 2), pl.ds(n * rows_q, rows_q)], ("qr", back))
    share_eigs.end()
    inverse[...] = 1.0 / (eigs_all[...].astype(f32) + damp)
    combine(1)
    train_y(3)
    multiply(3)
    queries = pairs.shape[0]
    lax.fori_loop(0, queries, scale, 0, unroll=2)
    for back in range(Z):
        at = position(back) * rows_g
        start = pl.multiple_of(step(me.z, -back, Z) * rows_g, rows_g)
        ts[:, at : at + rows_g] = sides[:, :, :, pl.ds(start, rows_g)].reshape(-1, rows_g)
    combine(2)
    train_y(4)
    multiply(4)
    combine(3)
    score((0, 1, 2))
    combine(4)
    score((3, 4))

    rows = tr.shape[1]
    row = lax.broadcasted_iota(jnp.int32, (rows, 128), 0)
    lane = lax.broadcasted_iota(jnp.int32, (rows, 128), 1)
    place = row // rows_g
    back = jnp.where(place % 2 == 1, (place + 1) // 2, Z - place // 2)
    z = (me.z + Z - back) % Z
    sample = (me.core * Y + (row % rows_g) // RANK) * Z + z
    sums = jnp.dot(
        pairs[...].reshape(-1, rows), jnp.where(lane == sample, 1.0, 0.0),
        preferred_element_type=f32, precision=lax.Precision.HIGHEST,
    )
    f1[me.g] = jnp.sum(sums.reshape(-1, 8, 128), axis=1)
    spread_group(net, "f1", f1)

    collect_group(net, "f1", f1)
    f2[me.y] = jnp.sum(f1[...], axis=0)
    spread_y(net, "f2", f2)
    collect_y(net, "f2", f2)
    f3[me.z] = jnp.sum(f2[...], axis=0)
    spread_z(net, "f3", f3)
    for back_z in range(Z):
        net.arrive(out_side.at[:, step(me.z, -back_z, Z)], ("swap_q", back_z), when=away)

    @pl.when(home)
    def _():
        out_side[...] = sides[:, :, :, cols:]

    collect_z(net, "f3", f3)
    part_sum[...] = jnp.sum(f3[...], axis=0)
    net.finish()


def precond_kernel(out_side, qr, eig_sum, part_sum, eigs, precond, scores, inv):
    turn = pl.program_id(0)
    x_lo = Place().x_lo
    each = precond.shape[0]

    @pl.when(turn == 0)
    def _():
        damp = (0.1 / (DS * DA)) * jnp.sum(eig_sum[...])
        inv[...] = 1.0 / (eigs[...] + damp)
        total = part_sum[:, : scores.shape[1]]
        scores[...] = total / jnp.sqrt(jnp.float32(RANK * DS * DA))

    for sub in range(each):
        query = turn * each + sub
        block = qr[x_lo]
        lane = lax.broadcasted_iota(jnp.int32, block.shape, 1)
        keep = jnp.logical_and(lane >= query * RANK, lane < (query + 1) * RANK)
        left = jnp.where(keep, block, 0.0).astype(jnp.bfloat16)
        precond[sub] = (nt(left, out_side[...]) * inv[...]).astype(jnp.bfloat16)


def precondition(out_side, qr, eig_sum, part_sum, eigs):
    queries = part_sum.shape[0]
    each = 2
    return pl.pallas_call(
        precond_kernel,
        grid=(queries // each,),
        out_shape=(
            jax.ShapeDtypeStruct((queries,) + eigs.shape, jnp.bfloat16),
            jax.ShapeDtypeStruct((queries, 2 * Y * Z), jnp.float32),
        ),
        in_specs=[VMEM] * 5,
        out_specs=(
            pl.BlockSpec((each,) + eigs.shape, lambda q: (q, 0, 0)),
            pl.BlockSpec((queries, 2 * Y * Z), lambda q: (0, 0)),
        ),
        scratch_shapes=[pltpu.VMEM(eigs.shape, jnp.float32)],
        compiler_params=pltpu.CompilerParams(vmem_limit_bytes=12 << 20),
        name="precondition",
    )(out_side, qr, eig_sum, part_sum, eigs)


def influence(train, basis, eigs, train_out, small, query_in, query_out, queries):
    bf16, f32 = jnp.bfloat16, jnp.float32
    rank, coords = train.shape
    block = basis.shape[0]
    wide = small.shape[1]
    width = wide // Y
    rows = Y * Z * rank
    query_rows = query_in.shape[0]
    rows_s = width // Z
    outer = (Z, rank, train_out.shape[1] // Z)
    return pl.pallas_call(
        rotate_kernel,
        out_shape=(
            jax.ShapeDtypeStruct((Y, Z, rows_s, query_rows), bf16),
            jax.ShapeDtypeStruct((2, block, query_rows), f32),
            jax.ShapeDtypeStruct((8, 128), f32),
            jax.ShapeDtypeStruct((queries, 128), f32),
        ),
        in_specs=[ANY] * 7,
        out_specs=[VMEM] * 4,
        scratch_shapes=[
            pltpu.VMEM((2 * block, rows), bf16),
            pltpu.VMEM((Y, Z, rows_s, rows + query_rows), bf16),
            pltpu.VMEM((2,) + eigs.shape, bf16),
            pltpu.VMEM(eigs.shape, bf16),
            pltpu.VMEM((2,) + eigs.shape, f32),
            pltpu.VMEM(train_out.shape, bf16),
            pltpu.VMEM(outer, bf16),
            pltpu.VMEM((queries, 2 * block, wide), bf16),
            pltpu.VMEM((wide, rows), bf16),
            pltpu.VMEM((queries, 8, rows), f32),
            pltpu.VMEM((GROUP, 8, 128), f32),
            pltpu.VMEM((Y, 8, 128), f32),
            pltpu.VMEM((Z, 8, 128), f32),
            pltpu.VMEM((Z, Y, rank, coords), bf16),
            pltpu.VMEM((2, block, coords), bf16),
            pltpu.VMEM((Z, Y) + outer[1:], bf16),
            pltpu.VMEM((2 * Y, small.shape[0], width), bf16),
            pltpu.VMEM((2 * Y * 128, width), bf16),
            pltpu.VMEM(basis.shape, bf16),
            pltpu.VMEM(query_in.shape, bf16),
            pltpu.VMEM((query_rows, 2 * Y * 128), bf16),
            pltpu.VMEM(eigs.shape, f32),
            pltpu.VMEM((2 * block, rows), bf16),
            pltpu.VMEM((X, 2 * block // X, rows), bf16),
            pltpu.VMEM((width, rows), bf16),
            pltpu.VMEM((Z, rows_s, rows), bf16),
            pltpu.VMEM((width, query_rows), f32),
            pltpu.VMEM((Z, rows_s, query_rows), f32),
            pltpu.VMEM((block, query_rows), f32),
            pltpu.VMEM((4, block // 4, query_rows), f32),
            pltpu.VMEM((GROUP, 8, 128), f32),
            pltpu.VMEM((Y, 8, 128), f32),
            pltpu.VMEM((Z, 8, 128), f32),
            pltpu.SemaphoreType.DMA((288,)),
            pltpu.SemaphoreType.DMA((288,)),
            pltpu.SemaphoreType.DMA((9 + 2 * Y,)),
        ],
        compiler_params=pltpu.CompilerParams(
            collective_id=0, has_side_effects=True, vmem_limit_bytes=58 << 20
        ),
        name="influence",
    )(train, basis, eigs, train_out, small, query_in, query_out)


def shards(query_in, query_out, train_in, train_out, basis_in, basis_out, eigvals):
    queries, qrank, coords = query_in.shape
    eigs = eigvals.T
    out_side, qr, eig_sum, part_sum = influence(
        train_in[0], basis_in, eigs, train_out[0], basis_out.T,
        query_in.reshape(queries * qrank, coords),
        query_out.reshape(queries * qrank, query_out.shape[2]), queries,
    )
    precond, scores = precondition(
        out_side.reshape(-1, out_side.shape[3]), qr, eig_sum, part_sum, eigs
    )
    return precond.transpose(0, 2, 1), scores


def solution(mesh):
    placed = (
        P(None, None, "narrow"),
        P(),
        P("wide", None, "narrow"),
        P("wide", None, None),
        P("wide", "narrow"),
        P("narrow", "wide"),
        P("narrow", "wide"),
    )
    return jax.shard_map(
        shards,
        mesh=mesh,
        in_specs=placed,
        out_specs=(P(None, "narrow", "wide"), P()),
        check_vma=False,
    )
```
